32 devices in a mesh: blk: 8 (over z, y), panel: 4 (over x, core).
Axes of the slice: x: 2, y: 2, z: 4, core: 2. Of those that a mesh axis runs over, the one named last changes fastest.
Arguments:
- left_env: bfloat16 [8, 80, 16128], P('blk', 'panel'), may hold values from -6 to 6
- right_env: bfloat16 [8, 80, 16128], P('blk', 'panel'), may hold values from -6 to 6
- site_tensors: bfloat16 [8, 80, 2304], P('blk', 'panel'), may hold values from -0.625 to 0.625
- chain_operator: bfloat16 [28, 28, 4, 4], replicated, may hold values from -0.5 to 0.5
- targets: int32 [8, 80], P('blk', 'panel'), may hold values from 0 to 79, as said below
- sector_dims: int32 [80], replicated, may hold values from 12 to 24
Outputs:
- left_out: bfloat16 [8, 80, 16128], P('blk', 'panel')
- right_out: bfloat16 [8, 80, 16128], P('blk', 'panel')
The draws below stay inside these ranges and needn't reach their ends.
Inputs may be any that keep to these rules, and one draw needn't show every extreme that they name: `targets`: for each site, sector p * 20 + j has right sector ((p + c_j) mod 4) * 20 + pi_j, with offsets c_j and a permutation pi of 20 slots that depend on the site only; each row is a permutation of the 80 sectors; each offset is taken by at most 10 slots, and one offset by exactly 10.
All inputs are finite; a program needn't handle non-finite values.
Results may differ from the reference program's by a relative error of at most 0.0076.
Values may be sent and summed in bfloat16 or wider, within the bound.
A program may use at most 64 MiB of HBM per device.

```python
import jax
import jax.numpy as jnp
from jax import lax

WD = 28
PHYS = 4
BLK = 24
SEC_DEV = 20
STEPS = 2
NSEC = 80
SITES = 8
CAP = 10


def draw_targets(key, part):
    key = jax.random.fold_in(key, 7)
    panels = NSEC // SEC_DEV

    def one_site(site_key):
        first_key, second_key, third_key = jax.random.split(site_key, 3)
        shuffled = jax.random.permutation(first_key, panels * CAP)
        busiest = jax.random.randint(second_key, (), 0, panels)
        others = (shuffled // CAP != busiest).astype(jnp.int32)
        ordering = jnp.argsort(others, stable=True)
        chosen = shuffled[ordering][:SEC_DEV]
        offsets = chosen // CAP
        landing = jax.random.permutation(third_key, SEC_DEV)
        owners = jnp.arange(panels)[:, None]
        mapped = (owners + offsets[None, :]) % panels * SEC_DEV + landing[None, :]
        return mapped.reshape(NSEC).astype(jnp.int32)
    return jax.vmap(one_site)(jax.random.split(key, SITES))


def touch_ends(result, stream_key, least, largest):
    longest = result.shape.index(max(result.shape))
    spots = []
    for shift in (0, 1):
        where = [jax.random.randint(jax.random.fold_in(stream_key, axis), (), 0, length) for axis, length in enumerate(result.shape)]
        where[longest] = (where[longest] + shift) % result.shape[longest]
        spots.append(tuple(where))
    return result.at[spots[0]].set(least).at[spots[1]].set(largest)


def level_of(key, extent, shards, low, high):
    gain = 1.0
    for position, blocks in shards:
        draws = jax.random.uniform(jax.random.fold_in(jax.random.fold_in(key, 6), position), (blocks,), jnp.float32, low / len(shards), high / len(shards))
        gain = gain * jnp.repeat(jnp.exp(draws), extent[position] // blocks).reshape((-1,) + (1,) * (len(extent) - 1 - position))
    return gain


def bell_draw(stream_key, extent, scale, limit, shards=(), dtype=jnp.bfloat16):
    drawn = scale * jax.random.normal(stream_key, extent, jnp.float32)
    if shards:
        drawn = drawn * level_of(stream_key, extent, shards, -0.22, 0.18)
    return jnp.clip(drawn, -limit, limit).astype(dtype)


def setup_inputs(seed: int = 0) -> dict:
    arg_keys = jax.random.split(jax.random.key(seed), 7)
    left_env = bell_draw(arg_keys[0], (SITES, NSEC, WD * BLK * BLK), 1.0, 6.0, ((0, 8), (1, 4)))
    right_env = bell_draw(arg_keys[1], (SITES, NSEC, WD * BLK * BLK), 1.0, 6.0, ((0, 8), (1, 4)))
    site_tensors = bell_draw(arg_keys[2], (SITES, NSEC, PHYS * BLK * BLK), (PHYS * BLK) ** -0.5, 0.625, ((0, 8), (1, 4)))
    chain_operator = bell_draw(arg_keys[3], (WD, WD, PHYS, PHYS), (WD * PHYS) ** -0.5, 0.5)
    targets = draw_targets(jax.random.fold_in(arg_keys[6], 71), 0)
    sector_dims = touch_ends(jax.random.randint(arg_keys[5], (NSEC,), BLK // 2, BLK + 1), jax.random.fold_in(arg_keys[5], 1), BLK // 2, BLK).astype(jnp.int32)
    return {"left_env": left_env, "right_env": right_env, "site_tensors": site_tensors, "chain_operator": chain_operator, "targets": targets, "sector_dims": sector_dims}


def masked(tensor, rows, cols):
    span = jnp.arange(BLK)
    keep_rows = (span[None, :] < rows[:, None])[:, None, :, None]
    keep_cols = (span[None, :] < cols[:, None])[:, None, None, :]
    keep = (keep_rows & keep_cols).astype(jnp.bfloat16)
    return tensor.reshape(-1, PHYS, BLK, BLK) * keep


def left_update(state, blocks, operator):
    count = state.shape[0]
    ket = state.reshape(count, WD, BLK, BLK).astype(jnp.float32)
    tensor = blocks.astype(jnp.float32)
    first = jnp.einsum('cwij,csjk->cwsik', ket, tensor).astype(jnp.bfloat16)
    second = jnp.einsum('wvts,cwsik->cvtik', operator.astype(jnp.float32), first.astype(jnp.float32)).astype(jnp.bfloat16)
    fresh = jnp.einsum('ctij,cvtik->cvjk', tensor, second.astype(jnp.float32)).astype(jnp.bfloat16)
    return fresh.reshape(count, -1)


def right_update(state, blocks, operator):
    count = state.shape[0]
    ket = state.reshape(count, WD, BLK, BLK).astype(jnp.float32)
    tensor = blocks.astype(jnp.float32)
    first = jnp.einsum('csij,cvjk->cvsik', tensor, ket).astype(jnp.bfloat16)
    second = jnp.einsum('wvts,cvsik->cwtik', operator.astype(jnp.float32), first.astype(jnp.float32)).astype(jnp.bfloat16)
    fresh = jnp.einsum('cwtik,ctjk->cwij', second.astype(jnp.float32), tensor).astype(jnp.bfloat16)
    return fresh.reshape(count, -1)


def reference(left_env, right_env, site_tensors, chain_operator, targets, sector_dims):
    def left_site(pieces):
        state, tensor, target = pieces
        blocks = masked(tensor, sector_dims, sector_dims[target])
        fresh = left_update(state, blocks, chain_operator)
        return jnp.zeros_like(fresh).at[target].set(fresh)

    def right_site(pieces):
        state, tensor, target = pieces
        blocks = masked(tensor, sector_dims, sector_dims[target])
        return right_update(state[target], blocks, chain_operator)

    left_now, right_now = left_env, right_env
    for turn_index in range(STEPS):
        left_now = jnp.roll(lax.map(left_site, (left_now, site_tensors, targets)), 1, axis=0)
        right_now = jnp.roll(lax.map(right_site, (right_now, site_tensors, targets)), -1, axis=0)
    return left_now, right_now
```

```python
import jax
import jax.numpy as jnp
from jax import lax
from jax.experimental import pallas as pl
from jax.experimental.pallas import tpu as pltpu
from jax.sharding import PartitionSpec as P

WD = 28
WPAD = 32
PHYS = 4
BLK = 24
GROUP = 5
LANES = 128
MID = WPAD * PHYS


def masked(tensor, rows, cols):
    span = jnp.arange(BLK)
    keep_rows = (span[None, :] < rows[:, None])[:, None, :, None]
    keep_cols = (span[None, :] < cols[:, None])[:, None, None, :]
    keep = (keep_rows & keep_cols).astype(jnp.bfloat16)
    return tensor.reshape(-1, PHYS, BLK, BLK) * keep


def pad_last(x, sizes):
    width = [(0, 0)] * (x.ndim - len(sizes))
    width += [(0, s - d) for s, d in zip(sizes, x.shape[x.ndim - len(sizes):])]
    return jnp.pad(x, width)


def lane_matrix(blocks):
    groups = blocks.shape[0] // GROUP
    x = blocks.reshape(groups, GROUP, PHYS, BLK, BLK).transpose(0, 1, 3, 2, 4)
    eye = jnp.eye(GROUP, dtype=bool)[None, :, None, None, :, None]
    x = jnp.where(eye, x[:, :, :, :, None, :], jnp.zeros((), jnp.bfloat16))
    x = x.reshape(groups, GROUP * BLK, PHYS, GROUP * BLK)
    x = jnp.pad(x, ((0, 0), (0, LANES - GROUP * BLK), (0, 0), (0, LANES - GROUP * BLK)))
    return x.reshape(groups, LANES, PHYS * LANES)


def row_matrix(blocks):
    groups = blocks.shape[0] // GROUP
    x = blocks.reshape(groups, GROUP, PHYS, BLK, BLK).transpose(0, 1, 4, 2, 3)
    return x.reshape(groups, GROUP * BLK, PHYS * BLK)


def operator_matrix(op):
    x = jnp.pad(op, ((0, WPAD - WD), (0, WPAD - WD), (0, 0), (0, 0)))
    return x.transpose(2, 0, 3, 1).reshape(MID, MID)


def update_kernel(env_ref, lane_ref, row_ref, op_ref, out_ref, x_ref, y_ref):
    rows = WD * BLK
    env = env_ref[0]
    for s in range(PHYS):
        x_ref[s, pl.ds(0, rows), :] = jnp.dot(
            env, lane_ref[0, :, s * LANES:(s + 1) * LANES], preferred_element_type=jnp.float32
        )
        x_ref[s, pl.ds(rows, (WPAD - WD) * BLK), :] = jnp.zeros(
            ((WPAD - WD) * BLK, LANES), jnp.float32
        )
    op = op_ref[...]
    for i in range(0, BLK, 2):
        parts = [
            jnp.concatenate(
                [x_ref[s, pl.ds(i + h, WPAD, stride=BLK), :] for s in range(PHYS)], axis=0
            )
            for h in range(2)
        ]
        both = jnp.concatenate(parts, axis=1).astype(jnp.bfloat16)
        y = jnp.dot(op, both, preferred_element_type=jnp.float32)
        for h in range(2):
            y_ref[pl.ds((i + h) * MID, MID), :] = y[:, h * LANES:(h + 1) * LANES]
    row = row_ref[0]
    owner = lax.broadcasted_iota(jnp.int32, (BLK, LANES), 1) // BLK
    for v in range(0, WD, 2):
        parts = [
            jnp.concatenate(
                [y_ref[pl.ds(t * WPAD + v + h, BLK, stride=MID), :] for t in range(PHYS)], axis=0
            )
            for h in range(2)
        ]
        both = jnp.concatenate(parts, axis=1).astype(jnp.bfloat16)
        z = jnp.dot(row, both, preferred_element_type=jnp.float32)
        for h in range(2):
            piece = z[:, h * LANES:(h + 1) * LANES]
            total = jnp.zeros((BLK, LANES), jnp.float32)
            for a in range(GROUP):
                total = jnp.where(owner == a, piece[a * BLK:(a + 1) * BLK], total)
            out_ref[0, pl.ds((v + h) * BLK, BLK), :] = total.astype(jnp.bfloat16)


def update(env, lane, row, op):
    groups = env.shape[0]
    rows = WD * BLK
    return pl.pallas_call(
        update_kernel,
        grid=(groups,),
        out_shape=jax.ShapeDtypeStruct((groups, rows, LANES), jnp.bfloat16),
        in_specs=[
            pl.BlockSpec((1, rows, LANES), lambda g: (g, 0, 0)),
            pl.BlockSpec((1, LANES, PHYS * LANES), lambda g: (g, 0, 0)),
            pl.BlockSpec((1, GROUP * BLK, PHYS * BLK), lambda g: (g, 0, 0)),
            pl.BlockSpec((MID, MID), lambda g: (0, 0)),
        ],
        out_specs=pl.BlockSpec((1, rows, LANES), lambda g: (g, 0, 0)),
        scratch_shapes=[
            pltpu.VMEM((PHYS, WPAD * BLK, LANES), jnp.float32),
            pltpu.VMEM((BLK * MID, LANES), jnp.float32),
        ],
        compiler_params=pltpu.CompilerParams(vmem_limit_bytes=32 * 1024 * 1024),
        cost_estimate=pl.CostEstimate(
            flops=groups * 2 * 128 * 128 * 128 * 72 * 20, bytes_accessed=16 << 20, transcendentals=0
        ),
    )(env, lane, row, op)


def to_lanes(state):
    groups = state.shape[0] // GROUP
    x = state.reshape(groups, GROUP, WD * BLK, BLK).transpose(0, 2, 1, 3)
    return pad_last(x.reshape(groups, WD * BLK, GROUP * BLK), (LANES,))


def from_lanes(x):
    groups = x.shape[0]
    x = x[:, :, : GROUP * BLK].reshape(groups, WD * BLK, GROUP, BLK)
    return x.transpose(0, 2, 1, 3).reshape(groups * GROUP, WD * BLK * BLK)


def shifted(x, by):
    length = lax.axis_size("blk")
    return lax.ppermute(x, "blk", [(i, (i + by) % length) for i in range(length)])


def gathered(x):
    panels = lax.axis_size("panel")
    me = lax.axis_index("panel")
    x = x[None]
    bit = panels // 2
    while bit:
        other = lax.ppermute(x, "panel", [(p, p ^ bit) for p in range(panels)])
        low = (me & bit) == 0
        x = jnp.stack([jnp.where(low, x, other), jnp.where(low, other, x)])
        x = x.reshape((-1,) + x.shape[2:])
        bit //= 2
    return x


def held_slot(panel, panels):
    slot = jnp.zeros_like(panel)
    bit = panels // 2
    place = 1
    while bit:
        slot = slot + jnp.where((panel & bit) != 0, place, 0)
        place *= 2
        bit //= 2
    return slot


def take_rows(held, index, per_device):
    panels = held.shape[0]
    slot = held_slot(index // per_device, panels) * per_device + index % per_device
    flat = held.reshape((panels * per_device,) + held.shape[2:])
    return jnp.take(flat, slot, axis=0, mode="clip")


def body(left_env, right_env, site_tensors, chain_operator, targets, sector_dims):
    per_device = left_env.shape[1]
    sites = lax.axis_size("blk")
    site = lax.axis_index("blk")
    panel = lax.axis_index("panel")
    sectors = sector_dims.shape[0]
    mine = panel * per_device + jnp.arange(per_device)

    right_far = gathered(shifted(right_env[0], -2))
    tensor_next = shifted(site_tensors[0], -1)
    tensor_far = gathered(tensor_next)
    tensor_two = gathered(shifted(site_tensors[0], -2))
    table = lax.all_gather(targets[0], ("blk", "panel"), tiled=True).reshape(sites, sectors)

    def row_of(offset):
        return jnp.take(table, (site + offset + sites) % sites, axis=0, mode="clip")

    reached = jnp.take(row_of(-1), row_of(-2), mode="clip")
    source = jnp.sum(
        jnp.where(reached[None, :] == mine[:, None], jnp.arange(sectors)[None, :], 0), axis=1
    )

    def site_pair(here, there, first_row, second_row):
        mid = jnp.take(first_row, mine, mode="clip")
        last = jnp.take(second_row, mid, mode="clip")
        dims = [jnp.take(sector_dims, x, mode="clip") for x in (mine, mid, last)]
        near = masked(here, dims[0], dims[1])
        far = masked(take_rows(there, mid, per_device), dims[1], dims[2])
        return near, far, last

    near, far, _ = site_pair(site_tensors[0], tensor_far, row_of(0), row_of(1))
    near_r, far_r, last = site_pair(tensor_next, tensor_two, row_of(1), row_of(2))
    near_t = near_r.transpose(0, 1, 3, 2)
    far_t = far_r.transpose(0, 1, 3, 2)
    left_op = operator_matrix(chain_operator.transpose(1, 0, 2, 3))
    right_op = operator_matrix(chain_operator.transpose(0, 1, 3, 2))

    left = to_lanes(left_env[0])
    left = update(left, lane_matrix(near), row_matrix(near), left_op)
    left = update(left, lane_matrix(far), row_matrix(far), left_op)
    left_far = gathered(shifted(from_lanes(left), 2))

    right = to_lanes(take_rows(right_far, last, per_device))
    right = update(right, lane_matrix(far_t), row_matrix(far_t), right_op)
    right = update(right, lane_matrix(near_t), row_matrix(near_t), right_op)
    right_out = from_lanes(right)

    left_out = take_rows(left_far, source, per_device)
    return (left_out[None], right_out[None])


def solution(mesh):
    placed = (
        P("blk", "panel", None),
        P("blk", "panel", None),
        P("blk", "panel", None),
        P(),
        P("blk", "panel"),
        P(),
    )
    return jax.shard_map(
        body,
        mesh=mesh,
        in_specs=placed,
        out_specs=(P("blk", "panel", None), P("blk", "panel", None)),
        check_vma=False,
    )
```

```python
import functools

import jax
import jax.numpy as jnp
import numpy as np
from jax import lax
from jax.experimental import pallas as pl
from jax.experimental.pallas import tpu as pltpu
from jax.sharding import PartitionSpec as P

WD = 28
WPAD = 32
PHYS = 4
BLK = 24
GROUP = 5
LANES = 128
MID = WPAD * PHYS


def masked(tensor, rows, cols):
    span = jnp.arange(BLK)
    keep_rows = (span[None, :] < rows[:, None])[:, None, :, None]
    keep_cols = (span[None, :] < cols[:, None])[:, None, None, :]
    keep = (keep_rows & keep_cols).astype(jnp.bfloat16)
    return tensor.reshape(-1, PHYS, BLK, BLK) * keep


def lane_matrix(blocks):
    groups = blocks.shape[0] // GROUP
    x = blocks.reshape(groups, GROUP, PHYS, BLK, BLK).transpose(0, 1, 3, 2, 4)
    return x.reshape(groups, GROUP * BLK, PHYS * BLK)


def row_matrix(blocks):
    groups = blocks.shape[0] // GROUP
    x = blocks.reshape(groups, GROUP, PHYS, BLK, BLK).transpose(0, 1, 4, 2, 3)
    return x.reshape(groups, GROUP * BLK, PHYS * BLK)


def spread_matrix():
    row = np.arange(PHYS * BLK)[:, None]
    col = np.arange(PHYS * LANES)[None, :]
    lane = col % LANES
    hit = (row // BLK == col // LANES) & (row % BLK == lane % BLK) & (lane < GROUP * BLK)
    return jnp.asarray(hit, jnp.bfloat16)


def operator_matrix(op):
    x = jnp.pad(op, ((0, WPAD - WD), (0, WPAD - WD), (0, 0), (0, 0)))
    return x.transpose(2, 0, 3, 1).reshape(MID, MID)


def update_kernel(
    first, env_ref, lane_ref, row_ref, op_ref, spread_ref, out_ref, e_ref, x_ref, y_ref, o_ref
):
    rows = WD * BLK
    spread = jnp.dot(lane_ref[0], spread_ref[...], preferred_element_type=jnp.float32)
    sector = lax.broadcasted_iota(jnp.int32, spread.shape, 0) // BLK
    place = lax.broadcasted_iota(jnp.int32, spread.shape, 1) % LANES // BLK
    lane = jnp.where(sector == place, spread, 0.0).astype(jnp.bfloat16)
    used = GROUP * BLK
    if first:
        e_ref[...] = jnp.zeros(e_ref.shape, e_ref.dtype)
        env = [env_ref[a].astype(jnp.float32) for a in range(GROUP)]
        for i in range(BLK):
            e_ref[pl.ds(i * WPAD, WD), pl.ds(0, used)] = jnp.concatenate(
                [x[:, i * BLK:(i + 1) * BLK] for x in env], axis=1
            )
        for s in range(PHYS):
            x_ref[s] = jnp.dot(
                e_ref[:, :used].astype(jnp.bfloat16),
                lane[:, s * LANES:(s + 1) * LANES],
                preferred_element_type=jnp.float32,
            )
    else:
        for s in range(PHYS):
            x_ref[s, pl.ds(0, rows), :] = jnp.dot(
                env_ref[0][:, :used],
                lane[:, s * LANES:(s + 1) * LANES],
                preferred_element_type=jnp.float32,
            )
            x_ref[s, pl.ds(rows, (WPAD - WD) * BLK), :] = jnp.zeros(
                ((WPAD - WD) * BLK, LANES), jnp.float32
            )

    def operator_rows(s, i):
        if first:
            return x_ref[s, pl.ds(i * WPAD, WPAD), :]
        return x_ref[s, pl.ds(i, WPAD, stride=BLK), :]

    op = op_ref[...]
    for i in range(0, BLK, 2):
        parts = [
            jnp.concatenate([operator_rows(s, i + h) for s in range(PHYS)], axis=0)
            for h in range(2)
        ]
        both = jnp.concatenate(parts, axis=1).astype(jnp.bfloat16)
        y = jnp.dot(op, both, preferred_element_type=jnp.float32)
        for h in range(2):
            y_ref[pl.ds((i + h) * MID, MID), :] = y[:, h * LANES:(h + 1) * LANES]
    row = row_ref[0]
    owner = lax.broadcasted_iota(jnp.int32, (BLK, LANES), 1) // BLK
    for v in range(0, WD, 2):
        parts = [
            jnp.concatenate(
                [y_ref[pl.ds(t * WPAD + v + h, BLK, stride=MID), :] for t in range(PHYS)], axis=0
            )
            for h in range(2)
        ]
        both = jnp.concatenate(parts, axis=1).astype(jnp.bfloat16)
        z = jnp.dot(row, both, preferred_element_type=jnp.float32)
        for h in range(2):
            piece = z[:, h * LANES:(h + 1) * LANES]
            total = jnp.zeros((BLK, LANES), jnp.float32)
            for a in range(GROUP):
                total = jnp.where(owner == a, piece[a * BLK:(a + 1) * BLK], total)
            where = pl.ds((v + h) * BLK, BLK)
            if first:
                out_ref[0, where, :] = total.astype(jnp.bfloat16)
            else:
                o_ref[where, :] = total
    if not first:
        wide = [o_ref[pl.ds(j, WD, stride=BLK), :] for j in range(BLK)]
        for a in range(GROUP):
            out_ref[a] = jnp.concatenate(
                [x[:, a * BLK:(a + 1) * BLK] for x in wide], axis=1
            ).astype(jnp.bfloat16)


def update(env, lane, row, op, first):
    groups = lane.shape[0]
    rows = WD * BLK
    flat = pl.BlockSpec((GROUP, WD, BLK * BLK), lambda g: (g, 0, 0))
    wide = pl.BlockSpec((1, rows, LANES), lambda g: (g, 0, 0))
    compact = pl.BlockSpec((1, GROUP * BLK, PHYS * BLK), lambda g: (g, 0, 0))
    return pl.pallas_call(
        functools.partial(update_kernel, first),
        grid=(groups,),
        out_shape=jax.ShapeDtypeStruct(
            (groups, rows, LANES) if first else (groups * GROUP, WD, BLK * BLK), jnp.bfloat16
        ),
        in_specs=[
            flat if first else wide,
            compact,
            compact,
            pl.BlockSpec((MID, MID), lambda g: (0, 0)),
            pl.BlockSpec((PHYS * BLK, PHYS * LANES), lambda g: (0, 0)),
        ],
        out_specs=wide if first else flat,
        scratch_shapes=[
            pltpu.VMEM((BLK * WPAD, LANES), jnp.float32),
            pltpu.VMEM((PHYS, WPAD * BLK, LANES), jnp.float32),
            pltpu.VMEM((BLK * MID, LANES), jnp.float32),
            pltpu.VMEM((rows, LANES), jnp.float32),
        ],
        compiler_params=pltpu.CompilerParams(vmem_limit_bytes=32 * 1024 * 1024),
        cost_estimate=pl.CostEstimate(
            flops=groups * 2 * 128 * 128 * 128 * 72 * 20, bytes_accessed=16 << 20, transcendentals=0
        ),
    )(env, lane, row, op, spread_matrix())


def two_updates(state, near, far, op):
    count = state.shape[0]
    mid = update(state.reshape(count, WD, BLK * BLK), near[0], near[1], op, True)
    return update(mid, far[0], far[1], op, False).reshape(count, -1)


def shifted(x, by):
    length = lax.axis_size("blk")
    return lax.ppermute(x, "blk", [(i, (i + by) % length) for i in range(length)])


def gathered(x):
    panels = lax.axis_size("panel")
    x = x[None]
    bit = panels // 2
    while bit:
        other = lax.ppermute(x, "panel", [(p, p ^ bit) for p in range(panels)])
        x = jnp.concatenate([x, other], axis=0)
        bit //= 2
    return x


def held_slot(panel):
    panels = lax.axis_size("panel")
    differ = panel ^ lax.axis_index("panel")
    slot = jnp.zeros_like(panel)
    bit = panels // 2
    place = 1
    while bit:
        slot = slot + jnp.where((differ & bit) != 0, place, 0)
        place *= 2
        bit //= 2
    return slot


def take_rows(held, index):
    per_device = held.shape[1]
    return held.at[held_slot(index // per_device), index % per_device].get(
        mode="promise_in_bounds"
    )


def body(left_env, right_env, site_tensors, chain_operator, targets, sector_dims):
    per_device = left_env.shape[1]
    panel = lax.axis_index("panel")
    mine = panel * per_device + jnp.arange(per_device)

    extra = jnp.stack([targets[0] // per_device, targets[0] % per_device], axis=1)
    own = jnp.concatenate(
        [site_tensors[0], jnp.pad(extra, ((0, 0), (0, LANES - 2))).astype(jnp.bfloat16)], axis=1
    )
    one, two = shifted(own, -1), shifted(own, -2)
    held = gathered(jnp.concatenate([one, two], axis=1))
    width = own.shape[1]
    size = site_tensors.shape[2]

    def sectors_of(rows):
        code = rows[:, size:size + 2].astype(jnp.int32)
        return code[:, 0] * per_device + code[:, 1]

    def site_pair(here, mid, there):
        last = sectors_of(there)
        dims = [jnp.take(sector_dims, x, mode="clip") for x in (mine, mid, last)]
        near = masked(here[:, :size], dims[0], dims[1])
        far = masked(there[:, :size], dims[1], dims[2])
        return near, far, last

    mid_l, mid_r = targets[0], sectors_of(one)
    near, far, last_l = site_pair(own, mid_l, take_rows(held, mid_l)[:, :width])
    near_r, far_r, last = site_pair(one, mid_r, take_rows(held, mid_r)[:, width:])
    reached = gathered(shifted(last_l, 2))

    right_far = gathered(shifted(right_env[0], -2))
    left_op = operator_matrix(chain_operator.transpose(1, 0, 2, 3))
    right_op = operator_matrix(chain_operator.transpose(0, 1, 3, 2))


    def left_pair(x):
        return lane_matrix(x), row_matrix(x)

    def right_pair(x):
        return row_matrix(x), lane_matrix(x)

    left = two_updates(left_env[0], left_pair(near), left_pair(far), left_op)
    left_far = gathered(shifted(left, 2))
    hits = reached.reshape(-1)[None, :] == mine[:, None]
    spot = jnp.sum(jnp.where(hits, jnp.arange(hits.shape[1])[None, :], 0), axis=1)

    right_out = two_updates(
        take_rows(right_far, last), right_pair(far_r), right_pair(near_r), right_op
    )
    left_out = left_far.at[spot // per_device, spot % per_device].get(mode="promise_in_bounds")
    return (left_out[None], right_out[None])


def solution(mesh):
    placed = (
        P("blk", "panel", None),
        P("blk", "panel", None),
        P("blk", "panel", None),
        P(),
        P("blk", "panel"),
        P(),
    )
    return jax.shard_map(
        body,
        mesh=mesh,
        in_specs=placed,
        out_specs=(P("blk", "panel", None), P("blk", "panel", None)),
        check_vma=False,
    )
```

```python
import functools

import jax
import jax.numpy as jnp
import numpy as np
from jax import lax
from jax.experimental import pallas as pl
from jax.experimental.pallas import tpu as pltpu
from jax.sharding import PartitionSpec as P

WD = 28
WPAD = 32
PHYS = 4
BLK = 24
GROUP = 5
LANES = 128
MID = WPAD * PHYS


def masked(tensor, rows, cols):
    span = jnp.arange(BLK)
    keep_rows = (span[None, :] < rows[:, None])[:, None, :, None]
    keep_cols = (span[None, :] < cols[:, None])[:, None, None, :]
    keep = (keep_rows & keep_cols).astype(jnp.bfloat16)
    return tensor.reshape(-1, PHYS, BLK, BLK) * keep


def site_layout(blocks, codes):
    x = blocks.transpose(0, 2, 1, 3).reshape(-1, BLK, PHYS * BLK)
    tail = jnp.pad(codes, ((0, 0), (0, LANES - PHYS * BLK - codes.shape[1])))
    tail = jnp.broadcast_to(tail[:, None, :], (x.shape[0], BLK, tail.shape[1]))
    return jnp.concatenate([x, tail.astype(jnp.bfloat16)], axis=2)


def spread_matrix():
    row = np.arange(PHYS * BLK)[:, None]
    col = np.arange(PHYS * LANES)[None, :]
    lane = col % LANES
    hit = (row // BLK == col // LANES) & (row % BLK == lane % BLK) & (lane < GROUP * BLK)
    return jnp.asarray(hit, jnp.bfloat16)


def operator_matrix(op):
    x = jnp.pad(op, ((0, WPAD - WD), (0, WPAD - WD), (0, 0), (0, 0)))
    return x.transpose(2, 0, 3, 1).reshape(MID, MID)


def update_kernel(
    first, flip, env_ref, site_ref, op_ref, spread_ref, out_ref, e_ref, x_ref, y_ref, o_ref
):
    rows = WD * BLK
    site = site_ref[...].reshape(GROUP * BLK, LANES)
    swapped = site.astype(jnp.float32).T
    turned = jnp.concatenate(
        [
            jnp.concatenate(
                [
                    swapped[t * BLK:(t + 1) * BLK, a * BLK:(a + 1) * BLK]
                    for t in range(PHYS)
                ],
                axis=1,
            )
            for a in range(GROUP)
        ],
        axis=0,
    ).astype(jnp.bfloat16)
    site = site[:, :PHYS * BLK]
    across, row = (turned, site) if flip else (site, turned)
    spread = jnp.dot(across, spread_ref[...], preferred_element_type=jnp.float32)
    sector = lax.broadcasted_iota(jnp.int32, spread.shape, 0) // BLK
    place = lax.broadcasted_iota(jnp.int32, spread.shape, 1) % LANES // BLK
    lane = jnp.where(sector == place, spread, 0.0).astype(jnp.bfloat16)
    used = GROUP * BLK
    if first:
        e_ref[...] = jnp.zeros(e_ref.shape, e_ref.dtype)
        env = [env_ref[a].astype(jnp.float32) for a in range(GROUP)]
        for i in range(BLK):
            e_ref[pl.ds(i * WPAD, WD), pl.ds(0, used)] = jnp.concatenate(
                [x[:, i * BLK:(i + 1) * BLK] for x in env], axis=1
            )
        for s in range(PHYS):
            x_ref[s] = jnp.dot(
                e_ref[:, :used].astype(jnp.bfloat16),
                lane[:, s * LANES:(s + 1) * LANES],
                preferred_element_type=jnp.float32,
            )
    else:
        for s in range(PHYS):
            x_ref[s, pl.ds(0, rows), :] = jnp.dot(
                env_ref[0][:, :used],
                lane[:, s * LANES:(s + 1) * LANES],
                preferred_element_type=jnp.float32,
            )
            x_ref[s, pl.ds(rows, (WPAD - WD) * BLK), :] = jnp.zeros(
                ((WPAD - WD) * BLK, LANES), jnp.float32
            )

    def operator_rows(s, i):
        if first:
            return x_ref[s, pl.ds(i * WPAD, WPAD), :]
        return x_ref[s, pl.ds(i, WPAD, stride=BLK), :]

    op = op_ref[...]
    for i in range(0, BLK, 2):
        parts = [
            jnp.concatenate([operator_rows(s, i + h) for s in range(PHYS)], axis=0)
            for h in range(2)
        ]
        both = jnp.concatenate(parts, axis=1).astype(jnp.bfloat16)
        y = jnp.dot(op, both, preferred_element_type=jnp.float32)
        for h in range(2):
            y_ref[pl.ds((i + h) * MID, MID), :] = y[:, h * LANES:(h + 1) * LANES]
    owner = lax.broadcasted_iota(jnp.int32, (BLK, LANES), 1) // BLK
    for v in range(0, WD, 2):
        parts = [
            jnp.concatenate(
                [y_ref[pl.ds(t * WPAD + v + h, BLK, stride=MID), :] for t in range(PHYS)], axis=0
            )
            for h in range(2)
        ]
        both = jnp.concatenate(parts, axis=1).astype(jnp.bfloat16)
        z = jnp.dot(row, both, preferred_element_type=jnp.float32)
        for h in range(2):
            piece = z[:, h * LANES:(h + 1) * LANES]
            total = jnp.zeros((BLK, LANES), jnp.float32)
            for a in range(GROUP):
                total = jnp.where(owner == a, piece[a * BLK:(a + 1) * BLK], total)
            where = pl.ds((v + h) * BLK, BLK)
            if first:
                out_ref[0, where, :] = total.astype(jnp.bfloat16)
            else:
                o_ref[where, :] = total
    if not first:
        wide = [o_ref[pl.ds(j, WD, stride=BLK), :] for j in range(BLK)]
        for a in range(GROUP):
            out_ref[a] = jnp.concatenate(
                [x[:, a * BLK:(a + 1) * BLK] for x in wide], axis=1
            ).astype(jnp.bfloat16)


def update(env, site, op, first, flip):
    groups = site.shape[0] // GROUP
    rows = WD * BLK
    flat = pl.BlockSpec((GROUP, WD, BLK * BLK), lambda g: (g, 0, 0))
    wide = pl.BlockSpec((1, rows, LANES), lambda g: (g, 0, 0))
    compact = pl.BlockSpec((GROUP, BLK, LANES), lambda g: (g, 0, 0))
    return pl.pallas_call(
        functools.partial(update_kernel, first, flip),
        grid=(groups,),
        out_shape=jax.ShapeDtypeStruct(
            (groups, rows, LANES) if first else (groups * GROUP, WD, BLK * BLK), jnp.bfloat16
        ),
        in_specs=[
            flat if first else wide,
            compact,
            pl.BlockSpec((MID, MID), lambda g: (0, 0)),
            pl.BlockSpec((PHYS * BLK, PHYS * LANES), lambda g: (0, 0)),
        ],
        out_specs=wide if first else flat,
        scratch_shapes=[
            pltpu.VMEM((BLK * WPAD, LANES), jnp.float32),
            pltpu.VMEM((PHYS, WPAD * BLK, LANES), jnp.float32),
            pltpu.VMEM((BLK * MID, LANES), jnp.float32),
            pltpu.VMEM((rows, LANES), jnp.float32),
        ],
        compiler_params=pltpu.CompilerParams(vmem_limit_bytes=32 * 1024 * 1024),
        cost_estimate=pl.CostEstimate(
            flops=groups * 2 * 128 * 128 * 128 * 72 * 20, bytes_accessed=16 << 20, transcendentals=0
        ),
    )(env, site, op, spread_matrix())


def two_updates(state, near, far, op, flip):
    count = state.shape[0]
    mid = update(state.reshape(count, WD, BLK * BLK), near, op, True, flip)
    return update(mid, far, op, False, flip).reshape(count, -1)


def pick_kernel(hit_ref, *refs):
    out_ref = refs[-1]
    total = jnp.dot(hit_ref[0], refs[0][...], preferred_element_type=jnp.float32)
    for number, ref in enumerate(refs[1:-1], 1):
        total += jnp.dot(hit_ref[number], ref[...], preferred_element_type=jnp.float32)
    out_ref[...] = total.astype(out_ref.dtype)


def picked(pieces, slot, row):
    count, width = pieces[0].shape
    held = jnp.arange(len(pieces))[:, None, None] == slot[None, :, None]
    hit = (held & (row[None, :, None] == jnp.arange(count)[None, None, :])).astype(jnp.bfloat16)
    step = width // 7
    block = pl.BlockSpec((count, step), lambda n: (0, n))
    return pl.pallas_call(
        pick_kernel,
        grid=(7,),
        out_shape=jax.ShapeDtypeStruct((count, width), pieces[0].dtype),
        in_specs=[pl.BlockSpec(hit.shape, lambda n: (0, 0, 0))] + [block] * len(pieces),
        out_specs=block,
        compiler_params=pltpu.CompilerParams(vmem_limit_bytes=32 * 1024 * 1024),
    )(hit, *pieces)


def shifted(x, by):
    length = lax.axis_size("blk")
    return lax.ppermute(x, "blk", [(i, (i + by) % length) for i in range(length)])


def gathered(x):
    panels = lax.axis_size("panel")
    x = x[None]
    bit = panels // 2
    while bit:
        other = lax.ppermute(x, "panel", [(p, p ^ bit) for p in range(panels)])
        x = jnp.concatenate([x, other], axis=0)
        bit //= 2
    return x


def held_slot(panel):
    panels = lax.axis_size("panel")
    differ = panel ^ lax.axis_index("panel")
    slot = jnp.zeros_like(panel)
    bit = panels // 2
    place = 1
    while bit:
        slot = slot + jnp.where((differ & bit) != 0, place, 0)
        place *= 2
        bit //= 2
    return slot


def pieces_of(x):
    panels = lax.axis_size("panel")
    held = [x]
    bit = panels // 2
    while bit:
        held += [lax.ppermute(y, "panel", [(p, p ^ bit) for p in range(panels)]) for y in held]
        bit //= 2
    return held


def body(left_env, right_env, site_tensors, chain_operator, targets, sector_dims):
    per_device = left_env.shape[1]
    panel = lax.axis_index("panel")
    mine = panel * per_device + jnp.arange(per_device)

    right_pieces = pieces_of(shifted(right_env[0], -2))

    mid_l = targets[0]
    codes = jnp.stack([mid_l // per_device, mid_l % per_device], axis=1)
    own = masked(
        site_tensors[0],
        jnp.take(sector_dims, mine, mode="clip"),
        jnp.take(sector_dims, mid_l, mode="clip"),
    )
    own = site_layout(own, codes)
    one, two = shifted(own, -1), shifted(own, -2)
    held = gathered(jnp.stack([one, two]))

    def sectors_of(rows):
        first = PHYS * BLK
        code = rows[:, 0, first:first + 2].astype(jnp.int32)
        return code[:, 0] * per_device + code[:, 1]

    def row_at(number, index):
        return held.at[held_slot(index // per_device), number, index % per_device].get(
            mode="promise_in_bounds"
        )

    mid_r = sectors_of(one)
    far_l, far_r = row_at(0, mid_l), row_at(1, mid_r)
    last_l, last_r = sectors_of(far_l), sectors_of(far_r)
    reached = gathered(shifted(last_l, 2))
    left_op = operator_matrix(chain_operator.transpose(1, 0, 2, 3))
    right_op = operator_matrix(chain_operator.transpose(0, 1, 3, 2))


    left_pieces = pieces_of(shifted(two_updates(left_env[0], own, far_l, left_op, False), 2))
    hits = reached.reshape(-1)[None, :] == mine[:, None]
    spot = jnp.sum(jnp.where(hits, jnp.arange(hits.shape[1])[None, :], 0), axis=1)

    right = picked(right_pieces, held_slot(last_r // per_device), last_r % per_device)
    right_out = two_updates(right, far_r, one, right_op, True)
    left_out = picked(left_pieces, spot // per_device, spot % per_device)
    return (left_out[None], right_out[None])


def solution(mesh):
    placed = (
        P("blk", "panel", None),
        P("blk", "panel", None),
        P("blk", "panel", None),
        P(),
        P("blk", "panel"),
        P(),
    )
    return jax.shard_map(
        body,
        mesh=mesh,
        in_specs=placed,
        out_specs=(P("blk", "panel", None), P("blk", "panel", None)),
        check_vma=False,
    )
```

```python
import functools

import jax
import jax.numpy as jnp
import numpy as np
from jax import lax
from jax.experimental import pallas as pl
from jax.experimental.pallas import tpu as pltpu
from jax.sharding import PartitionSpec as P

WD = 28
WPAD = 32
PHYS = 4
BLK = 24
GROUP = 5
LANES = 128
MID = WPAD * PHYS


def masked(tensor, rows, cols):
    span = jnp.arange(BLK)
    keep_rows = (span[None, :] < rows[:, None])[:, None, :, None]
    keep_cols = (span[None, :] < cols[:, None])[:, None, None, :]
    keep = (keep_rows & keep_cols).astype(jnp.bfloat16)
    return tensor.reshape(-1, PHYS, BLK, BLK) * keep


def site_layout(blocks, codes):
    x = blocks.transpose(0, 2, 1, 3).reshape(-1, BLK, PHYS * BLK)
    tail = jnp.pad(codes, ((0, 0), (0, LANES - PHYS * BLK - codes.shape[1])))
    tail = jnp.broadcast_to(tail[:, None, :], (x.shape[0], BLK, tail.shape[1]))
    return jnp.concatenate([x, tail.astype(jnp.bfloat16)], axis=2)


def spread_matrix():
    row = np.arange(PHYS * BLK)[:, None]
    col = np.arange(PHYS * LANES)[None, :]
    lane = col % LANES
    hit = (row // BLK == col // LANES) & (row % BLK == lane % BLK) & (lane < GROUP * BLK)
    return jnp.asarray(hit, jnp.bfloat16)


def operator_matrix(op):
    x = jnp.pad(op, ((0, WPAD - WD), (0, WPAD - WD), (0, 0), (0, 0)))
    return x.transpose(2, 0, 3, 1).reshape(MID, MID)


def update_kernel(
    first, flip, env_ref, site_ref, op_ref, spread_ref, out_ref, e_ref, x_ref, y_ref, o_ref
):
    rows = WD * BLK
    site = site_ref[...].reshape(GROUP * BLK, LANES)
    swapped = site.astype(jnp.float32).T
    turned = jnp.concatenate(
        [
            jnp.concatenate(
                [
                    swapped[t * BLK:(t + 1) * BLK, a * BLK:(a + 1) * BLK]
                    for t in range(PHYS)
                ],
                axis=1,
            )
            for a in range(GROUP)
        ],
        axis=0,
    ).astype(jnp.bfloat16)
    site = site[:, :PHYS * BLK]
    across, row = (turned, site) if flip else (site, turned)
    spread = jnp.dot(across, spread_ref[...], preferred_element_type=jnp.float32)
    sector = lax.broadcasted_iota(jnp.int32, spread.shape, 0) // BLK
    place = lax.broadcasted_iota(jnp.int32, spread.shape, 1) % LANES // BLK
    lane = jnp.where(sector == place, spread, 0.0).astype(jnp.bfloat16)
    used = GROUP * BLK
    if first:
        e_ref[...] = jnp.zeros(e_ref.shape, e_ref.dtype)
        env = [env_ref[a].astype(jnp.float32) for a in range(GROUP)]
        for i in range(BLK):
            e_ref[pl.ds(i * WPAD, WD), pl.ds(0, used)] = jnp.concatenate(
                [x[:, i * BLK:(i + 1) * BLK] for x in env], axis=1
            )
        for s in range(PHYS):
            x_ref[s] = jnp.dot(
                e_ref[:, :used].astype(jnp.bfloat16),
                lane[:, s * LANES:(s + 1) * LANES],
                preferred_element_type=jnp.float32,
            )
    else:
        for s in range(PHYS):
            x_ref[s, pl.ds(0, rows), :] = jnp.dot(
                env_ref[0][:, :used],
                lane[:, s * LANES:(s + 1) * LANES],
                preferred_element_type=jnp.float32,
            )
            x_ref[s, pl.ds(rows, (WPAD - WD) * BLK), :] = jnp.zeros(
                ((WPAD - WD) * BLK, LANES), jnp.float32
            )

    def operator_rows(s, i):
        if first:
            return x_ref[s, pl.ds(i * WPAD, WPAD), :]
        return x_ref[s, pl.ds(i, WPAD, stride=BLK), :]

    op = op_ref[...]
    for i in range(0, BLK, 2):
        parts = [
            jnp.concatenate([operator_rows(s, i + h) for s in range(PHYS)], axis=0)
            for h in range(2)
        ]
        both = jnp.concatenate(parts, axis=1).astype(jnp.bfloat16)
        y = jnp.dot(op, both, preferred_element_type=jnp.float32)
        for h in range(2):
            y_ref[pl.ds((i + h) * MID, MID), :] = y[:, h * LANES:(h + 1) * LANES]
    owner = lax.broadcasted_iota(jnp.int32, (BLK, LANES), 1) // BLK
    for v in range(0, WD, 2):
        parts = [
            jnp.concatenate(
                [y_ref[pl.ds(t * WPAD + v + h, BLK, stride=MID), :] for t in range(PHYS)], axis=0
            )
            for h in range(2)
        ]
        both = jnp.concatenate(parts, axis=1).astype(jnp.bfloat16)
        z = jnp.dot(row, both, preferred_element_type=jnp.float32)
        for h in range(2):
            piece = z[:, h * LANES:(h + 1) * LANES]
            total = jnp.zeros((BLK, LANES), jnp.float32)
            for a in range(GROUP):
                total = jnp.where(owner == a, piece[a * BLK:(a + 1) * BLK], total)
            where = pl.ds((v + h) * BLK, BLK)
            if first:
                out_ref[0, where, :] = total.astype(jnp.bfloat16)
            else:
                o_ref[where, :] = total
    if not first:
        wide = [o_ref[pl.ds(j, WD, stride=BLK), :] for j in range(BLK)]
        for a in range(GROUP):
            out_ref[a] = jnp.concatenate(
                [x[:, a * BLK:(a + 1) * BLK] for x in wide], axis=1
            ).astype(jnp.bfloat16)


def update(env, site, op, first, flip):
    groups = site.shape[0] // GROUP
    rows = WD * BLK
    flat = pl.BlockSpec((GROUP, WD, BLK * BLK), lambda g: (g, 0, 0))
    wide = pl.BlockSpec((1, rows, LANES), lambda g: (g, 0, 0))
    compact = pl.BlockSpec((GROUP, BLK, LANES), lambda g: (g, 0, 0))
    return pl.pallas_call(
        functools.partial(update_kernel, first, flip),
        grid=(groups,),
        out_shape=jax.ShapeDtypeStruct(
            (groups, rows, LANES) if first else (groups * GROUP, WD, BLK * BLK), jnp.bfloat16
        ),
        in_specs=[
            flat if first else wide,
            compact,
            pl.BlockSpec((MID, MID), lambda g: (0, 0)),
            pl.BlockSpec((PHYS * BLK, PHYS * LANES), lambda g: (0, 0)),
        ],
        out_specs=wide if first else flat,
        scratch_shapes=[
            pltpu.VMEM((BLK * WPAD, LANES), jnp.float32),
            pltpu.VMEM((PHYS, WPAD * BLK, LANES), jnp.float32),
            pltpu.VMEM((BLK * MID, LANES), jnp.float32),
            pltpu.VMEM((rows, LANES), jnp.float32),
        ],
        compiler_params=pltpu.CompilerParams(vmem_limit_bytes=32 * 1024 * 1024),
        cost_estimate=pl.CostEstimate(
            flops=groups * 2 * 128 * 128 * 128 * 72 * 20, bytes_accessed=16 << 20, transcendentals=0
        ),
    )(env, site, op, spread_matrix())


def two_updates(state, near, far, op, flip):
    count = state.shape[0]
    mid = update(state.reshape(count, WD, BLK * BLK), near, op, True, flip)
    return update(mid, far, op, False, flip).reshape(count, -1)


def pick_kernel(parts, hit_ref, *refs):
    out_ref = refs[-1]
    count = (len(refs) - 1) // parts

    for part in range(parts):
        @pl.when(pl.program_id(0) == part)
        def _():
            total = jnp.zeros(out_ref.shape, jnp.float32)
            for number, ref in enumerate(refs[part * count:(part + 1) * count]):
                total += jnp.dot(hit_ref[number], ref[...], preferred_element_type=jnp.float32)
            out_ref[...] = total.astype(out_ref.dtype)


def picked(parts, slot, row):
    steps = 7
    count, width = parts[0][0].shape
    panels = len(parts[0])
    held = jnp.arange(panels)[:, None, None] == slot[None, :, None]
    hit = (held & (row[None, :, None] == jnp.arange(count)[None, None, :])).astype(jnp.bfloat16)
    step = width // steps

    def place(part):
        return lambda h, n: (0, jnp.where(h == part, n, jnp.where(h < part, 0, steps - 1)))

    blocks = [pl.BlockSpec((count, step), place(part)) for part in range(len(parts))]
    return pl.pallas_call(
        functools.partial(pick_kernel, len(parts)),
        grid=(len(parts), steps),
        out_shape=jax.ShapeDtypeStruct((count, len(parts) * width), parts[0][0].dtype),
        in_specs=[pl.BlockSpec(hit.shape, lambda h, n: (0, 0, 0))]
        + [block for block in blocks for _ in range(panels)],
        out_specs=pl.BlockSpec((count, step), lambda h, n: (0, h * steps + n)),
        compiler_params=pltpu.CompilerParams(vmem_limit_bytes=32 * 1024 * 1024),
    )(hit, *[piece for part in parts for piece in part])


def shifted(x, by):
    length = lax.axis_size("blk")
    return lax.ppermute(x, "blk", [(i, (i + by) % length) for i in range(length)])


def gathered(x):
    panels = lax.axis_size("panel")
    x = x[None]
    bit = panels // 2
    while bit:
        other = lax.ppermute(x, "panel", [(p, p ^ bit) for p in range(panels)])
        x = jnp.concatenate([x, other], axis=0)
        bit //= 2
    return x


def held_slot(panel):
    panels = lax.axis_size("panel")
    differ = panel ^ lax.axis_index("panel")
    slot = jnp.zeros_like(panel)
    bit = panels // 2
    place = 1
    while bit:
        slot = slot + jnp.where((differ & bit) != 0, place, 0)
        place *= 2
        bit //= 2
    return slot


def pieces_of(x):
    panels = lax.axis_size("panel")
    held = [x]
    bit = panels // 2
    while bit:
        held += [lax.ppermute(y, "panel", [(p, p ^ bit) for p in range(panels)]) for y in held]
        bit //= 2
    return held


def body(left_env, right_env, site_tensors, chain_operator, targets, sector_dims):
    per_device = left_env.shape[1]
    panel = lax.axis_index("panel")
    mine = panel * per_device + jnp.arange(per_device)

    right_pieces = pieces_of(shifted(right_env[0], -2))

    mid_l = targets[0]
    codes = jnp.stack([mid_l // per_device, mid_l % per_device], axis=1)
    own = masked(
        site_tensors[0],
        jnp.take(sector_dims, mine, mode="clip"),
        jnp.take(sector_dims, mid_l, mode="clip"),
    )
    own = site_layout(own, codes)
    one, two = shifted(own, -1), shifted(own, -2)
    held = gathered(jnp.stack([one, two]))

    def sectors_of(rows):
        first = PHYS * BLK
        code = rows[:, 0, first:first + 2].astype(jnp.int32)
        return code[:, 0] * per_device + code[:, 1]

    def row_at(number, index):
        return held.at[held_slot(index // per_device), number, index % per_device].get(
            mode="promise_in_bounds"
        )

    mid_r = sectors_of(one)
    far_l, far_r = row_at(0, mid_l), row_at(1, mid_r)
    last_l, last_r = sectors_of(far_l), sectors_of(far_r)
    reached = gathered(shifted(last_l, 2))
    left_op = operator_matrix(chain_operator.transpose(1, 0, 2, 3))
    right_op = operator_matrix(chain_operator.transpose(0, 1, 3, 2))


    left = two_updates(left_env[0], own, far_l, left_op, False)
    half = left.shape[1] // 2
    front = shifted(left[:, :half], 2)
    front, back = lax.optimization_barrier((front, left[:, half:]))
    left_parts = [pieces_of(front), pieces_of(shifted(back, 2))]
    hits = reached.reshape(-1)[None, :] == mine[:, None]
    spot = jnp.sum(jnp.where(hits, jnp.arange(hits.shape[1])[None, :], 0), axis=1)

    right = picked([right_pieces], held_slot(last_r // per_device), last_r % per_device)
    right_out = two_updates(right, far_r, one, right_op, True)
    left_out = picked(left_parts, spot // per_device, spot % per_device)
    return (left_out[None], right_out[None])


def solution(mesh):
    placed = (
        P("blk", "panel", None),
        P("blk", "panel", None),
        P("blk", "panel", None),
        P(),
        P("blk", "panel"),
        P(),
    )
    return jax.shard_map(
        body,
        mesh=mesh,
        in_specs=placed,
        out_specs=(P("blk", "panel", None), P("blk", "panel", None)),
        check_vma=False,
    )
```
